32 devices in a mesh: dp: 8 (over y, x, core), vocab: 4 (over z).
Axes of the slice: x: 2, y: 2, z: 4, core: 2. Of those that a mesh axis runs over, the one named last changes fastest.
Arguments:
- code_ids: int32 [96, 256], P(('dp', 'vocab')), may hold values from 0 to 1023
- masked: int32 [96, 256], P(('dp', 'vocab')), may hold values from 0 to 1, as said below
- labels: int32 [96], P(('dp', 'vocab')), may hold values from 0 to 999
- dropped: int32 [96], P(('dp', 'vocab')), may hold values 0 or 1
- owners: int32 [24], replicated, may hold values from 0 to 7, as said below
- step_count: int32 [1], replicated, may hold values from 2 to 20
- master_block_weight: float32 [32, 768, 768], P('dp'), may hold values from -0.21875 to 0.21875
- matrix_first_moment: float32 [32, 768, 768], P('dp'), may hold values from -0.00061035156 to 0.00061035156
- matrix_second_moment: float32 [32, 768, 768], P('dp'), may hold values from 5.859375e-09 to 2.4820963e-08
- embed_weight: float32 [1024, 768], P('vocab'), may hold values from -0.875 to 0.875
- embed_first: float32 [1024, 768], P('vocab'), may hold values from -0.00061035156 to 0.00061035156
- embed_second: float32 [1024, 768], P('vocab'), may hold values from 5.859375e-09 to 2.4820963e-08
- extra_weight: float32 [1259, 768], replicated, may hold values from -6 to 6
- extra_first: float32 [1259, 768], replicated, may hold values from -0.00061035156 to 0.00061035156
- extra_second: float32 [1259, 768], replicated, may hold values from 5.859375e-09 to 2.4820963e-08
- norm_weight: float32 [10, 768], replicated, may hold values from -1.5 to 1.5
- norm_first: float32 [10, 768], replicated, may hold values from -0.00061035156 to 0.00061035156
- norm_second: float32 [10, 768], replicated, may hold values from 5.859375e-09 to 2.4820963e-08
- bias_weight: float32 [1024], replicated, may hold values from -6 to 6
- bias_first: float32 [1024], replicated, may hold values from -0.00061035156 to 0.00061035156
- bias_second: float32 [1024], replicated, may hold values from 5.859375e-09 to 2.4820963e-08
Outputs:
- step_loss: float32 [], replicated
- new_block_weight: float32 [32, 768, 768], P('dp')
- new_block_first: float32 [32, 768, 768], P('dp')
- new_block_second: float32 [32, 768, 768], P('dp')
- new_embed_weight: float32 [1024, 768], P('vocab')
- new_embed_first: float32 [1024, 768], P('vocab')
- new_embed_second: float32 [1024, 768], P('vocab')
- new_extra_weight: float32 [1259, 768], replicated
- new_extra_first: float32 [1259, 768], replicated
- new_extra_second: float32 [1259, 768], replicated
- new_norm_weight: float32 [10, 768], replicated
- new_norm_first: float32 [10, 768], replicated
- new_norm_second: float32 [10, 768], replicated
- new_bias_weight: float32 [1024], replicated
- new_bias_first: float32 [1024], replicated
- new_bias_second: float32 [1024], replicated
The draws below stay inside these ranges and needn't reach their ends.
Inputs may be any that keep to these rules, and one draw needn't show every extreme that they name: Every image has 1 to 256 masked codes. `owners`: no owner holds more than 4 matrices, and some owner holds exactly 4.
All inputs are finite; a program needn't handle non-finite values. No bound on the sum of `dropped` on one device may be relied on, other than what follows from the above.
Results may differ from the reference program's by a relative error of at most 0.0096.
Values may be sent and summed in bfloat16 or wider, within the bound.
A program may use at most 384 MiB of HBM per device.

```python
import math
import jax
import jax.numpy as jnp
import numpy as np
from jax import lax

MODEL_WIDTH = 768
HEADS = 8
HEAD_DIM = 96
FF = 3072
CODES = 1024
CLASSES = 1000
IMAGE_TOKENS = 256
LAYERS = 2
BLOCKS = 24
SLOTS_PER_OWNER = 4
OWNER_SLOTS = 32
IMAGE_TOTAL = 96
EXTRA = 1259
NORMS = 10
N_DP = 8


def row_order(row_key):
    return jax.random.permutation(row_key, IMAGE_TOKENS)


def draw_masked(key, part):
    base = jax.random.fold_in(key, 11)
    key_counts, key_orders = jax.random.split(base)
    masked_counts = jax.random.randint(key_counts, (IMAGE_TOTAL, 1), 1, IMAGE_TOKENS + 1)
    position_ranks = jax.vmap(row_order)(jax.random.split(key_orders, IMAGE_TOTAL))
    return (position_ranks < masked_counts).astype(jnp.int32)


def draw_owners(key, part):
    base = jax.random.fold_in(key, 23)
    key_sorted_order, key_owner_rank, key_shuffle = jax.random.split(base, 3)
    sampled_scores = jax.random.permutation(key_sorted_order, OWNER_SLOTS)
    slot_numbers = jnp.arange(OWNER_SLOTS)
    selected_entries = jax.random.randint(key_owner_rank, (), 0, OWNER_SLOTS // SLOTS_PER_OWNER)
    ranked = jnp.where(slot_numbers // SLOTS_PER_OWNER == selected_entries, slot_numbers % SLOTS_PER_OWNER - SLOTS_PER_OWNER, sampled_scores)
    picked = jnp.argsort(ranked, stable=True)[:BLOCKS]
    picked = jax.random.permutation(key_shuffle, picked)
    return (picked // SLOTS_PER_OWNER).astype(jnp.int32)


def with_ends(values, stream_key, smallest, high):
    shape = values.shape
    spot = [jax.random.randint(jax.random.fold_in(stream_key, axis), (), 0, shape[axis]) for axis in range(len(shape))]
    values = values.at[tuple(spot)].set(smallest)
    longest = shape.index(max(shape))
    spot[longest] = (spot[longest] + 1) % shape[longest]
    return values.at[tuple(spot)].set(high)


def steps_of(own_key, shape, cuts, least, high):
    def one(position, parts):
        steps = jax.random.uniform(jax.random.fold_in(jax.random.fold_in(own_key, 6), position), (parts,), jnp.float32, least / len(cuts), high / len(cuts))
        return jnp.repeat(jnp.exp(steps), shape[position] // parts).reshape((-1,) + (1,) * (len(shape) - position - 1))

    level = one(*cuts[0])
    for cut in cuts[1:]:
        level = level * one(*cut)
    return level


def rank_bounds(number_of, skew):
    weights = [(1 << 20) // math.isqrt(standing ** skew) + 1 for standing in range(1, number_of + 1)]
    scale = 1 + sum(weights) // (1 << 30)
    return np.cumsum(np.array([max(1, weight // scale) for weight in weights]))


def skewed_ids(own_key, extent, number_of, skew):
    grid = rank_bounds(number_of, skew)
    ticket = jax.random.randint(jax.random.fold_in(own_key, 1), extent, 0, int(grid[number_of - 1]))
    rank = jnp.searchsorted(jnp.asarray(grid, jnp.int32), ticket, side="right")
    return jax.random.permutation(jax.random.fold_in(own_key, 2), number_of)[rank].astype(jnp.int32)


def bell_draw(own_key, shape, deviation, bound, cuts=(), dtype=jnp.bfloat16):
    drawn = jax.random.normal(own_key, shape, jnp.float32) * deviation
    if len(cuts) > 0:
        drawn = steps_of(own_key, shape, cuts, -0.22, 0.18) * drawn
    return jnp.clip(drawn, min=-bound, max=bound).astype(dtype)


def setup_inputs(seed: int = 0) -> dict:
    splits = jax.random.split(jax.random.key(seed), 22)
    return {
        "code_ids": with_ends(jax.random.randint(splits[0], (IMAGE_TOTAL, IMAGE_TOKENS), 0, CODES), jax.random.fold_in(splits[0], 1), 0, CODES - 1).astype(jnp.int32),
        "masked": draw_masked(jax.random.fold_in(splits[21], 71), 0),
        "labels": with_ends(skewed_ids(splits[2], (IMAGE_TOTAL,), CLASSES, 2), jax.random.fold_in(splits[2], 3), 0, CLASSES - 1).astype(jnp.int32),
        "dropped": with_ends((jax.random.randint(splits[3], (IMAGE_TOTAL,), 0, 10) < 1).astype(jnp.int32), jax.random.fold_in(splits[3], 1), 0, 1),
        "owners": draw_owners(jax.random.fold_in(splits[21], 71), 0),
        "step_count": jax.random.randint(splits[5], (1,), 2, 21).astype(jnp.int32),
        "master_block_weight": bell_draw(splits[6], (OWNER_SLOTS, MODEL_WIDTH, MODEL_WIDTH), MODEL_WIDTH ** -0.5, 0.21875, ((0, 8),), jnp.float32),
        "matrix_first_moment": bell_draw(splits[7], (OWNER_SLOTS, MODEL_WIDTH, MODEL_WIDTH), (0.0066 * (IMAGE_TOTAL * IMAGE_TOKENS) ** -0.5), 0.00061035156, ((0, 8),), jnp.float32),
        "matrix_second_moment": jnp.clip(jnp.exp(math.log(2.4820963062666124e-08) - 1.4436456 * jax.random.uniform(splits[8], (OWNER_SLOTS, MODEL_WIDTH, MODEL_WIDTH), jnp.float32) ** steps_of(splits[8], (OWNER_SLOTS, MODEL_WIDTH, MODEL_WIDTH), ((0, 8),), -0.2, 0.2)), 5.859375207251105e-09, 2.4820963062666124e-08),
        "embed_weight": bell_draw(splits[9], (CODES, MODEL_WIDTH), 0.06, 0.875, ((0, 4),), jnp.float32),
        "embed_first": bell_draw(splits[10], (CODES, MODEL_WIDTH), (0.0066 * (IMAGE_TOTAL * IMAGE_TOKENS) ** -0.5), 0.00061035156, ((0, 4),), jnp.float32),
        "embed_second": jnp.clip(jnp.exp(math.log(2.4820963062666124e-08) - 1.4436456 * jax.random.uniform(splits[11], (CODES, MODEL_WIDTH), jnp.float32) ** steps_of(splits[11], (CODES, MODEL_WIDTH), ((0, 4),), -0.2, 0.2)), 5.859375207251105e-09, 2.4820963062666124e-08),
        "extra_weight": bell_draw(splits[12], (EXTRA, MODEL_WIDTH), 1.0, 6.0, (), jnp.float32),
        "extra_first": bell_draw(splits[13], (EXTRA, MODEL_WIDTH), (0.0066 * (IMAGE_TOTAL * IMAGE_TOKENS) ** -0.5), 0.00061035156, (), jnp.float32),
        "extra_second": jnp.clip(jnp.exp(jax.random.uniform(splits[14], (EXTRA, MODEL_WIDTH), jnp.float32, math.log(5.859375207251105e-09), math.log(2.4820963062666124e-08))), 5.859375207251105e-09, 2.4820963062666124e-08),
        "norm_weight": jnp.clip(jax.random.uniform(splits[15], (NORMS, MODEL_WIDTH), jnp.float32, -1.5, 1.5), -1.5, 1.5),
        "norm_first": bell_draw(splits[16], (NORMS, MODEL_WIDTH), (0.0066 * (IMAGE_TOTAL * IMAGE_TOKENS) ** -0.5), 0.00061035156, (), jnp.float32),
        "norm_second": jnp.clip(jnp.exp(jax.random.uniform(splits[17], (NORMS, MODEL_WIDTH), jnp.float32, math.log(5.859375207251105e-09), math.log(2.4820963062666124e-08))), 5.859375207251105e-09, 2.4820963062666124e-08),
        "bias_weight": bell_draw(splits[18], (CODES,), 0.5, 6.0, (), jnp.float32),
        "bias_first": bell_draw(splits[19], (CODES,), (0.0066 * (IMAGE_TOTAL * IMAGE_TOKENS) ** -0.5), 0.00061035156, (), jnp.float32),
        "bias_second": jnp.clip(jnp.exp(jax.random.uniform(splits[20], (CODES,), jnp.float32, math.log(5.859375207251105e-09), math.log(2.4820963062666124e-08))), 5.859375207251105e-09, 2.4820963062666124e-08),
    }


@jax.custom_vjp
def low(v):
    return lax.optimization_barrier(v.astype(jnp.bfloat16)).astype(jnp.float32)

@jax.custom_vjp
def low_back(v):
    return v

def low_keep(v):
    return (low(v), None)

def low_pass(kept, grad):
    return (grad,)

def back_keep(v):
    return (v, None)

def back_low(kept, grad):
    return (low(grad),)
low.defvjp(low_keep, low_pass)
low_back.defvjp(back_keep, back_low)
NORM_EPS = 1e-05
BETA_ONE = 0.9
BETA_TWO = 0.96
ADAM_EPS = 1e-08
DECAY = 0.045
HIGHEST_PRECISION = lax.Precision.HIGHEST

def rounded(inputs):
    return low(low_back(inputs))

def norm_rows(inputs, norm_gain, norm_shift):
    row_mean = lax.optimization_barrier(jnp.mean(inputs, -1, keepdims=True))
    centred = inputs - row_mean
    spread = lax.optimization_barrier(jnp.mean(centred * centred, -1, keepdims=True))
    return centred * lax.rsqrt(spread + NORM_EPS) * norm_gain + norm_shift

def product(left_side, right_side):
    return jnp.einsum('...d,de->...e', left_side, right_side, precision=HIGHEST_PRECISION)

def layer_forward(stream, layer_weights, norm_gains):
    images, seq_len, width = stream.shape
    pieces = FF // MODEL_WIDTH
    attn_in = low(norm_rows(stream, norm_gains[0], norm_gains[1]))
    queries = rounded(product(attn_in, layer_weights[0])).reshape(images, seq_len, HEADS, HEAD_DIM)
    key_heads = rounded(product(attn_in, layer_weights[1])).reshape(images, seq_len, HEADS, HEAD_DIM)
    value_heads = rounded(product(attn_in, layer_weights[2])).reshape(images, seq_len, HEADS, HEAD_DIM)
    scores = low_back(jnp.einsum('bqhd,bkhd->bhqk', queries, key_heads, precision=HIGHEST_PRECISION) * HEAD_DIM ** (-0.5))
    attn_probs = low(jax.nn.softmax(scores, axis=-1))
    attended = rounded(jnp.einsum('bhqk,bkhd->bqhd', attn_probs, value_heads, precision=HIGHEST_PRECISION).reshape(images, seq_len, width))
    middle = stream + low_back(product(attended, layer_weights[3]))
    mlp_in = low(norm_rows(middle, norm_gains[2], norm_gains[3]))
    up_weight = jnp.concatenate([layer_weights[4 + j] for j in range(pieces)], axis=1)
    up_proj = low_back(product(mlp_in, up_weight))
    hidden = low(jax.nn.gelu(up_proj, approximate=False))
    down_weight = jnp.concatenate([layer_weights[4 + pieces + j] for j in range(pieces)], axis=0)
    return middle + low_back(product(hidden, down_weight))

def group_loss(params, code_ids, masked, classes, inverse):
    blocks, embed, extra, norms, head_bias = params
    all_weights = low(blocks)
    code_table = low(embed)
    per_layer = BLOCKS // LAYERS
    mask_float = masked.astype(jnp.float32)[..., None]
    code_rows = jnp.where(mask_float > 0, extra[IMAGE_TOKENS + 1], math.sqrt(MODEL_WIDTH) * code_table[code_ids])
    class_rows = extra[IMAGE_TOKENS + 2 + classes]
    tokens = low_back(jnp.concatenate([class_rows[:, None], code_rows], axis=1))
    stream = tokens + extra[:IMAGE_TOKENS + 1]
    for layer_index in range(LAYERS):
        stream = layer_forward(stream, all_weights[per_layer * layer_index:per_layer * (layer_index + 1)], norms[4 * layer_index:4 * layer_index + 4])
    final_rows = low(norm_rows(stream, norms[4 * LAYERS], norms[4 * LAYERS + 1]))[:, 1:].reshape(-1, MODEL_WIDTH)
    flat_codes = code_ids.reshape(-1)
    logits = low_back(product(final_rows, code_table.T)) + head_bias
    log_total = jax.nn.logsumexp(logits, axis=-1)
    target_logit = lax.optimization_barrier(jnp.sum(final_rows * code_table[flat_codes], -1)) + head_bias[flat_codes]
    return jnp.sum(masked.reshape(-1).astype(jnp.float32) * (log_total - target_logit)) * inverse

def adam_update(weight, moment_one, moment_two, gradient, step_rate, step_float):
    moment_one = BETA_ONE * moment_one + (1.0 - BETA_ONE) * gradient
    moment_two = BETA_TWO * moment_two + (1.0 - BETA_TWO) * gradient * gradient
    fix_one = 1.0 - BETA_ONE ** step_float
    fix_two = 1.0 - BETA_TWO ** step_float
    weight = weight - step_rate * (moment_one / fix_one / (jnp.sqrt(moment_two / fix_two) + ADAM_EPS) + DECAY * weight)
    return (weight, moment_one, moment_two)

def reference(code_ids, masked, labels, dropped, owners, step_count, master_block_weight, matrix_first_moment, matrix_second_moment, embed_weight, embed_first, embed_second, extra_weight, extra_first, extra_second, norm_weight, norm_first, norm_second, bias_weight, bias_first, bias_second):
    block_index = jnp.arange(BLOCKS)
    same_owner = (owners[None, :] == owners[:, None]) & (block_index[None, :] < block_index[:, None])
    owner_rank = lax.optimization_barrier(jnp.sum(same_owner.astype(jnp.int32), axis=1)).astype(jnp.int32)
    slot_of = (owners * SLOTS_PER_OWNER + owner_rank).astype(jnp.int32)
    classes = jnp.where(dropped == 1, CLASSES, labels).astype(jnp.int32)
    inverse = 1.0 / jnp.sum(masked.astype(jnp.float32))
    per_group = IMAGE_TOTAL // N_DP
    batch_arrays = (code_ids.reshape(N_DP, per_group, IMAGE_TOKENS), masked.reshape(N_DP, per_group, IMAGE_TOKENS), classes.reshape(N_DP, per_group))
    checked_loss = jax.checkpoint(group_loss)

    def total_loss(params):

        def add_group(carry_sum, group_arrays):
            return (carry_sum + checked_loss(params, group_arrays[0], group_arrays[1], group_arrays[2], inverse), None)
        summed, unused = lax.scan(add_group, jnp.zeros((), jnp.float32), batch_arrays)
        return summed
    params = (master_block_weight[slot_of], embed_weight, extra_weight, norm_weight, bias_weight)
    step_loss, pull_back = jax.vjp(total_loss, params)
    gradients = pull_back(jnp.ones_like(step_loss))[0]
    step_float = step_count[0].astype(jnp.float32)
    new_blocks = adam_update(master_block_weight[slot_of], matrix_first_moment[slot_of], matrix_second_moment[slot_of], gradients[0], 0.03, step_float)
    block_out = [jnp.zeros_like(master_block_weight).at[slot_of].set(item) for item in new_blocks]
    table_out = adam_update(embed_weight, embed_first, embed_second, gradients[1], 0.05, step_float)
    extra_out = adam_update(extra_weight, extra_first, extra_second, gradients[2], 0.5, step_float)
    norm_out = adam_update(norm_weight, norm_first, norm_second, gradients[3], 0.5, step_float)
    bias_out = adam_update(bias_weight, bias_first, bias_second, gradients[4], 0.3, step_float)
    return (step_loss, block_out[0], block_out[1], block_out[2], table_out[0], table_out[1], table_out[2], extra_out[0], extra_out[1], extra_out[2], norm_out[0], norm_out[1], norm_out[2], bias_out[0], bias_out[1], bias_out[2])
```

```python
import functools
import math

import jax
import jax.numpy as jnp
from jax import lax
from jax.experimental import pallas as pl
from jax.experimental.pallas import tpu as pltpu
from jax.sharding import PartitionSpec as P

MODEL_WIDTH = 768
HEADS = 8
HEAD_DIM = 96
FF = 3072
CODES = 1024
CLASSES = 1000
IMAGE_TOKENS = 256
LAYERS = 2
BLOCKS = 24


NORM_EPS = 1e-05
BETA_ONE = 0.9
BETA_TWO = 0.96
ADAM_EPS = 1e-08
DECAY = 0.045


MESH = pl.DeviceIdType.MESH
W = 768
HALF = 384
BF = jnp.bfloat16
F32 = jnp.float32

def place():
    d = lax.axis_index("dp")
    k = lax.axis_index("vocab")
    q = d % 2
    x = (d // 2) % 2
    y = d // 4
    chip_x = y * 2 + (1 - x)
    chip_y = (1 - y) * 2 + x
    chip_d = (1 - y) * 2 + (1 - x)
    return d, k, q, d // 2, chip_x, chip_y, chip_d

def barrier(d, k):
    sem = pltpu.get_barrier_semaphore()
    for i in range(1, 8):
        pl.semaphore_signal(sem, inc=1, device_id=((d + i) % 8, k), device_id_type=MESH)
    for i in range(1, 4):
        pl.semaphore_signal(sem, inc=1, device_id=(d, (k + i) % 4), device_id_type=MESH)
    pl.semaphore_wait(sem, 10)

def remote(src, dst, s, r, dd, kk):
    return pltpu.make_async_remote_copy(src_ref=src, dst_ref=dst, send_sem=s, recv_sem=r, device_id=(dd, kk), device_id_type=MESH)

def rows(lo, n):
    return pl.ds(pl.multiple_of(lo, 16), n)

def half(q):
    return pl.ds(pl.multiple_of(q * HALF, HALF), HALF)

SEQ = 272
REAL = 257
ROWS = 3 * SEQ
SCALE = HEAD_DIM ** (-0.5)
WINDOW = ((0, 1), (0, 2), (1, 3), (2, 3), (3, 4), (3, 5), (4, 6), (5, 6))

def dot(a, b):
    return jnp.dot(a, b, preferred_element_type=F32)

def dot_tb(a, b):
    return lax.dot_general(a, b, (((1,), (1,)), ((), ())), preferred_element_type=F32)

def dot_ta(a, b):
    return lax.dot_general(a, b, (((0,), (0,)), ((), ())), preferred_element_type=F32)

def loop(n, fn):
    lax.fori_loop(0, n, lambda i, _: (fn(i), 0)[1], 0)

def row_chunk(i):
    return pl.ds(pl.multiple_of(i * 48, 16), 48)

def normed(x):
    centred = x - jnp.mean(x, -1, keepdims=True)
    rstd = lax.rsqrt(jnp.mean(centred * centred, -1, keepdims=True) + NORM_EPS)
    return centred * rstd, rstd

def norm_into(out, x, norm_ref, row):
    def one(i):
        r = row_chunk(i)
        out[r] = (normed(x[r])[0] * norm_ref[row:row + 1] + norm_ref[row + 1:row + 2]).astype(BF)
    loop(ROWS // 48, one)

def gelu_terms(u):
    cdf = 0.5 * (1.0 + lax.erf(u * 2.0 ** -0.5))
    return u * cdf, cdf + u * jnp.exp(-0.5 * u * u) * (2.0 * math.pi) ** -0.5

def head_mask(h):
    lo, hi = WINDOW[h]
    lane = lax.broadcasted_iota(jnp.int32, (SEQ, (hi - lo) * 128), 1) + lo * 128
    return (lane >= HEAD_DIM * h) & (lane < HEAD_DIM * (h + 1)), slice(lo * 128, hi * 128)

def join_heads(ref, r, base, o, scale=1.0):
    ref[r, base:base + 128] = ((o[0] + o[1][:, :128]) * scale).astype(BF)
    ref[r, base + 128:base + 256] = ((o[1][:, 128:] + o[2][:, :128]) * scale).astype(BF)
    ref[r, base + 256:base + 384] = ((o[2][:, 128:] + o[3]) * scale).astype(BF)

def attend(i, q, k, v, att, probs):
    r = pl.ds(pl.multiple_of(i * SEQ, 16), SEQ)
    real = lax.broadcasted_iota(jnp.int32, (SEQ, SEQ), 1) < REAL
    zero = jnp.zeros((), BF)
    for base in range(2):
        outs = []
        for h in range(4 * base, 4 * base + 4):
            m, cs = head_mask(h)
            s = jnp.where(real, dot_tb(jnp.where(m, q[r, cs], zero), k[r, cs]), -1e30)
            e = jnp.exp((s - jnp.max(s, axis=1, keepdims=True)) * SCALE)
            p = (e * (1.0 / jnp.sum(e, axis=1, keepdims=True))).astype(BF)
            probs[i, h] = p
            outs.append(dot(p, jnp.where(m, v[r, cs], zero)))
        join_heads(att, r, 384 * base, outs)

def attend_back(base, i, q, k, v, probs, do, dq, dk, dv):
    r = pl.ds(pl.multiple_of(i * SEQ, 16), SEQ)
    zero = jnp.zeros((), BF)
    oq, ok, ov = [], [], []
    for h in range(4 * base, 4 * base + 4):
        m, cs = head_mask(h)
        p = probs[i, h]
        dom = jnp.where(m, do[r, cs], zero)
        pf = p.astype(F32)
        w = pf * dot_tb(dom, v[r, cs])
        ds = (w - pf * jnp.sum(w, axis=1, keepdims=True)).astype(BF)
        oq.append(dot(ds, jnp.where(m, k[r, cs], zero)))
        ok.append(dot_ta(ds, jnp.where(m, q[r, cs], zero)))
        ov.append(dot_ta(p, dom))
    join_heads(dq, r, 384 * base, oq, SCALE)
    join_heads(dk, r, 384 * base, ok, SCALE)
    join_heads(dv, r, 384 * base, ov)

class Moves:
    def __init__(self, sems):
        self.sems, self.index, self.busy = sems, {}, {}
    def start(self, name, src, dst):
        self.free(name)
        i = self.index.setdefault(name, len(self.index))
        self.busy[name] = pltpu.make_async_copy(src, dst, self.sems.at[i])
        self.busy[name].start()
    def free(self, *names):
        for n in names or list(self.busy):
            if n in self.busy:
                self.busy.pop(n).wait()

class Weights:
    def __init__(self, moves, wall, ring, order, ready=lambda b: None):
        self.moves, self.wall, self.ring, self.order, self.ready = moves, wall, ring, order, ready
        self.slots, self.next, self.used = ring.shape[0], 0, 0
    def fill(self, ahead):
        while self.next < min(len(self.order), self.used + ahead):
            b = self.order[self.next]
            self.ready(b)
            s = self.next % self.slots
            self.moves.start(("w", s), self.wall.at[b], self.ring.at[s])
            self.next += 1
    def take(self, b):
        assert self.order[self.used] == b
        self.fill(1)
        s = self.used % self.slots
        self.moves.free(("w", s))
        self.used += 1
        self.fill(self.slots - 1)
        return self.ring.at[s]

def is_late(b):
    return b >= 6 and b % 2 == 1

class Gatherer:
    def __init__(self, at, wall, chunk, sems):
        self.d, self.k, self.q, self.c, self.cx, self.cy, self.cd = at
        self.wall, self.chunk, self.sems = wall, chunk, sems
        self.kp = self.k % 2
        self.peer = self.k + 1 - 2 * self.kp
        self.xn, self.yn, self.partner = self.cx * 2 + self.q, self.cy * 2 + self.q, self.c * 2 + (1 - self.q)
        self.cols = half(self.q)
        self.sent, self.own = {}, []
        self.nxy = self.nfw = self.nco = self.nzl = 0
    def send(self, stage, b, j, src, dst, dd, kk):
        i = b * 8 + stage + j
        cp = remote(src, dst, self.sems.at[0, i], self.sems.at[1, i], dd, kk)
        cp.start()
        self.sent.setdefault((b, stage), []).append(cp)
    def arrived(self, b, stage):
        for cp in self.sent[b, stage]:
            cp.wait_recv()
    def move(self, stage, b, j, reg, dd):
        self.send(stage, b, j, reg, reg, dd, self.k)
    def begin(self, own_sems):
        for b in range(24):
            dst = self.wall.at[b, self.c, self.kp, :, self.cols]
            o = pltpu.make_async_copy(self.chunk.at[b], dst, own_sems.at[b])
            o.start()
            self.own.append(o)
            if not is_late(b):
                self.send(0, b, 0, self.chunk.at[b], dst, self.d, self.peer)
    def xy(self, b):
        self.own[b].wait()
        if is_late(b):
            reg = self.wall.at[b, self.c, self.kp, :, self.cols]
        else:
            self.arrived(b, 0)
            reg = self.wall.at[b, self.c, :, :, self.cols]
        self.move(1, b, 0, reg, self.xn)
        self.move(1, b, 1, reg, self.yn)
    def fw(self, b):
        self.arrived(b, 1)
        if is_late(b):
            self.move(3, b, 0, self.wall.at[b, self.cx, self.kp, pl.ds(0, 48), self.cols], self.yn)
            self.move(3, b, 1, self.wall.at[b, self.cy, self.kp, pl.ds(48, 48), self.cols], self.xn)
        else:
            self.move(3, b, 0, self.wall.at[b, self.cx, 0, :, self.cols], self.yn)
            self.move(3, b, 1, self.wall.at[b, self.cy, 1, :, self.cols], self.xn)
    def zl(self, b):
        if is_late(b):
            self.arrived(b, 3)
            reg = self.wall.at[b, :, self.kp, :, self.cols]
            self.send(5, b, 0, reg, reg, self.d, self.peer)
    def co(self, b):
        self.arrived(b, 5 if is_late(b) else 3)
        self.move(6, b, 0, self.wall.at[b, :, :, :, self.cols], self.partner)
    def advance(self, nxy, nfw, nzl, nco):
        while self.nxy < min(nxy, 24):
            self.xy(self.nxy)
            self.nxy += 1
        while self.nfw < min(nfw, 24):
            self.fw(self.nfw)
            self.nfw += 1
        while self.nzl < min(nzl, 24):
            self.zl(self.nzl)
            self.nzl += 1
        while self.nco < min(nco, 24):
            self.co(self.nco)
            self.nco += 1
    def finish(self):
        for cps in self.sent.values():
            for cp in cps:
                cp.wait_send()

AHEAD = ((2, 1, 1, 0), (8, 5, 3, 1))

def forward_kernel(slot_ref, send_ref, table_ref, count_ref, ids_ref, mask_ref, pos_ref, few_ref, norm_ref,
                   wall, full_ref, total_ref, stream0, stream1, stream2, middles, lns, qkvs, atts, probs_out, hids, slopes,
                   st, mid, up, ln, qkv, att, probs, hid, slope, ring, sems, slots, chunk, cnt, own_sems, g_sems,
                   a2a_s, a2a_r, t_s, t_r, tp_s, tp_r, tc_s, tc_r, n_s, n_r, np_s, np_r):
    at = place()
    d, k, q, c, cx, cy, cd = at
    ga = Gatherer(at, wall, chunk, g_sems)
    cols = ga.cols
    xn, yn, dn, partner = ga.xn, ga.yn, cd * 2 + q, ga.partner
    barrier(d, k)
    mv = Moves(sems)
    started = []
    def go(cp):
        cp.start()
        started.append(cp)
        return cp
    trow = rows(k * 256 + c * 64, 64)
    tz = [go(remote(table_ref.at[rows(c * 64, 64), cols], full_ref.at[trow, cols], t_s.at[i], t_r.at[i], d, (k + i) % 4)) for i in range(1, 4)]
    nz = [go(remote(count_ref, cnt.at[k, d], n_s.at[i], n_r.at[i], d, (k + i) % 4)) for i in range(1, 4)]
    a2a = []
    for i in range(1, 8):
        t = (d + i) % 8
        a2a.append(go(remote(send_ref.at[:, t // 2, :, half(t % 2)], slots.at[d], a2a_s.at[i], a2a_r.at[i], t, k)))
    mv.start("mine", send_ref.at[:, c, :, cols], slots.at[d])
    mv.start("tmine", table_ref, full_ref.at[rows(k * 256, 256)])
    cnt[k, d] = count_ref[...]
    for cp in tz:
        cp.wait_recv()
    tps = []
    for i in range(1, 4):
        rr = full_ref.at[rows(((k + i) % 4) * 256 + c * 64, 64), cols]
        for j, t in enumerate((xn, yn, dn)):
            tps.append(go(remote(rr, rr, tp_s.at[i, j], tp_r.at[i, j], t, k)))
    for cp in nz:
        cp.wait_recv()
    npl = [go(remote(cnt.at[:, d], cnt.at[:, d], np_s.at[i], np_r.at[i], (d + i) % 8, k)) for i in range(1, 8)]
    for i in range(3):
        def base(j, i=i):
            r, p = pl.ds(pl.multiple_of(SEQ * i + j * 16, 16), 16), pl.ds(pl.multiple_of(j * 16, 16), 16)
            st[r] = pos_ref[p] + mask_ref[r] * few_ref[3:4]
        loop(17, base)
        st[SEQ * i + 256:SEQ * i + 257] = pos_ref[256:257] + few_ref[i:i + 1]
    mv.free("mine")
    for cp in a2a:
        cp.wait_recv()
    for b in range(24):
        s = slot_ref[b]
        chunk[b] = slots[s // 4, s % 4]
    ga.begin(own_sems)
    mv.free("tmine")
    for cp in tps:
        cp.wait_recv()
    tcs = []
    for i in range(1, 4):
        rr = full_ref.at[rows(((k + i) % 4) * 256, 256), cols]
        tcs.append(go(remote(rr, rr, tc_s.at[i], tc_r.at[i], partner, k)))
    ga.advance(3, 0, 0, 0)
    for cp in npl:
        cp.wait_recv()
    total_ref[...] = jnp.sum(cnt[...], axis=(0, 1))
    for cp in tcs:
        cp.wait_recv()
    hot = (lax.broadcasted_iota(jnp.int32, (ROWS, CODES), 1) == ids_ref[...]).astype(BF)
    for n in range(3):
        cs = slice(256 * n, 256 * n + 256)
        st[:, cs] = st[:, cs] + math.sqrt(MODEL_WIDTH) * dot(hot, full_ref[:, cs])
    mv.start("st", st, stream0)
    nslots = ring.shape[0]
    def step(t):
        lo, hi = AHEAD
        n = [min(a + t, b) for a, b in zip(lo, hi)]
        ga.advance(*(t + 1 + x for x in n))
    def fetch(b):
        if b < 24:
            step(b)
            ga.arrived(b, 6)
            mv.start(("w", b % nslots), wall.at[b], ring.at[b % nslots])
    def weight(b, n):
        if n == 0:
            mv.free(("w", b % nslots))
        if n == 1:
            fetch(b + 1)
        return ring[b % nslots, :, :, :, 256 * n:256 * n + 256].reshape(W, 256)
    ga.advance(3, 1, 0, 0)
    for l in range(LAYERS):
        base = 12 * l
        mv.free("st")
        if l:
            mv.start("st", st, stream1)
        mv.free("ln0")
        norm_into(ln.at[0], st, norm_ref, 4 * l)
        mv.start("ln0", ln.at[0], lns.at[l, 0])
        if l == 0:
            fetch(0)
        for j in range(3):
            mv.free(("qkv", j))
            for n in range(3):
                cs = slice(256 * n, 256 * n + 256)
                qkv[j, :, cs] = dot(ln[0], weight(base + j, n)).astype(BF)
            mv.start(("qkv", j), qkv.at[j], qkvs.at[l, j])
        mv.free("att", "probs")
        loop(3, lambda i: attend(i, qkv.at[0], qkv.at[1], qkv.at[2], att, probs))
        mv.start("att", att, atts.at[l])
        mv.start("probs", probs, probs_out.at[l])
        mv.free("mid")
        for n in range(3):
            cs = slice(256 * n, 256 * n + 256)
            mid[:, cs] = st[:, cs] + dot(att[...], weight(base + 3, n))
        mv.start("mid", mid, middles.at[l])
        mv.free("ln1")
        norm_into(ln.at[1], mid, norm_ref, 4 * l + 2)
        mv.start("ln1", ln.at[1], lns.at[l, 1])
        for j in range(4):
            for n in range(3):
                cs = slice(256 * n, 256 * n + 256)
                up[:, cs] = dot(ln[1], weight(base + 4 + j, n))
            mv.free(("hid", j), ("slope", j))
            def gelu(i, j=j):
                r = row_chunk(i)
                h, g = gelu_terms(up[r])
                hid[j, r] = h.astype(BF)
                slope[j, r] = g.astype(BF)
            loop(ROWS // 48, gelu)
            mv.start(("hid", j), hid.at[j], hids.at[l, j])
            mv.start(("slope", j), slope.at[j], slopes.at[l, j])
        mv.free("st")
        for j in range(4):
            for n in range(3):
                cs = slice(256 * n, 256 * n + 256)
                st[:, cs] = (st if j else mid)[:, cs] + dot(hid[j], weight(base + 8 + j, n))
    mv.start("st", st, stream2)
    ga.finish()
    for cp in started:
        cp.wait_send()
    mv.free()

def forward(slot_of, send, table, count, ids, mask, pos, few, norms):
    S = jax.ShapeDtypeStruct
    V = pltpu.VMEM
    D = pltpu.SemaphoreType.DMA
    any_ = pl.BlockSpec(memory_space=pl.ANY)
    vm = pl.BlockSpec(memory_space=pltpu.VMEM)
    shapes = (S((24, 4, 2, 96, W), BF), S((CODES, W), BF), S((8, 128), F32), S((ROWS, W), F32),
              S((ROWS, W), F32), S((ROWS, W), F32), S((2, ROWS, W), F32), S((2, 2, ROWS, W), BF), S((2, 3, ROWS, W), BF),
              S((2, ROWS, W), BF), S((2, 3, 8, SEQ, SEQ), BF), S((2, 4, ROWS, W), BF), S((2, 4, ROWS, W), BF))
    f32 = V((ROWS, W), F32)
    return pl.pallas_call(
        forward_kernel, out_shape=shapes,
        in_specs=[pl.BlockSpec(memory_space=pltpu.SMEM), any_, any_] + [vm] * 6, out_specs=(any_, vm, vm) + (any_,) * 10,
        scratch_shapes=[f32, f32, f32, V((2, ROWS, W), BF), V((3, ROWS, W), BF), V((ROWS, W), BF),
                        V((3, 8, SEQ, SEQ), BF), V((4, ROWS, W), BF), V((4, ROWS, W), BF), V((3, 4, 2, 96, W), BF), D((32,)),
                        V((8, 4, 96, HALF), BF), V((24, 96, HALF), BF), V((4, 8, 8, 128), F32), D((24,)), D((2, 192)),
                        D((8,)), D((8,)), D((4,)), D((4,)), D((4, 3)), D((4, 3)), D((4,)), D((4,)), D((4,)), D((4,)), D((8,)), D((8,))],
        compiler_params=pltpu.CompilerParams(collective_id=0, has_side_effects=True, vmem_limit_bytes=60 * 2**20),
        cost_estimate=pl.CostEstimate(flops=24 * 2 * ROWS * W * W, bytes_accessed=100 * 10**6, transcendentals=10**7),
        name="layers",
    )(slot_of, send, table, count, ids, mask, pos, few, norms)

def chunks_to_send(master):
    part = master.reshape(4, 4, 2, 96, W)
    return lax.dynamic_index_in_dim(part, lax.axis_index("vocab") % 2, 2, keepdims=False).astype(BF)

def norm_back(x, dy, add, out, norm_ref, row, dnorm):
    def one(i, carry):
        r = row_chunk(i)
        xhat, rstd = normed(x[r])
        g = dy[r]
        a = g * norm_ref[row:row + 1]
        out[r] = add[r] + rstd * (a - jnp.mean(a, -1, keepdims=True) - xhat * jnp.mean(a * xhat, -1, keepdims=True))
        return (carry[0] + jnp.sum((g * xhat).reshape(6, 8, W), 0), carry[1] + jnp.sum(g.reshape(6, 8, W), 0))
    zero = jnp.zeros((8, W), F32)
    gain, shift = lax.fori_loop(0, ROWS // 48, one, (zero, zero))
    dnorm[row:row + 1] = jnp.sum(gain, 0, keepdims=True)
    dnorm[row + 1:row + 2] = jnp.sum(shift, 0, keepdims=True)

def round_into(out, x):
    def one(i):
        out[row_chunk(i)] = x[row_chunk(i)].astype(BF)
    loop(ROWS // 48, one)

LAGS = (1, 3, 5, 7, 9)

class Reducer:
    def __init__(self, mv, at, dring, sums, tmps, vv, land, sems):
        self.mv, self.dring, self.sums, self.vv, self.sems = mv, dring, sums, vv, sems
        self.d, self.k, self.q, self.c, self.cx, self.cy, self.cd = at
        self.tc, self.td, self.te, self.tf = tmps
        self.cb, self.dv, self.ev, self.f1, self.f2 = land
        q = self.q
        self.xn, self.yn, self.partner = self.cx * 2 + q, self.cy * 2 + q, self.c * 2 + (1 - q)
        self.kp = self.k % 2
        self.peer, self.cross = self.k + 1 - 2 * self.kp, (self.k + 2) % 4
        self.mine, self.other = half(q), half(1 - q)
        self.sent, self.blocks, self.born, self.n = {}, [], [], 0
    def send(self, stage, u, j, src, dst, dd, kk):
        i = u * 8 + stage + j
        cp = remote(src, dst, self.sems.at[0, i], self.sems.at[1, i], dd, kk)
        cp.start()
        self.sent.setdefault((u, stage), []).append(cp)
    def arrived(self, u, stage):
        for cp in self.sent[u, stage]:
            cp.wait_recv()
    def gone(self, u, *stages):
        for s in stages:
            for cp in self.sent[u, s]:
                cp.wait_send()
    def slot(self):
        n = len(self.blocks)
        s = n % self.dring.shape[0]
        if n >= self.dring.shape[0]:
            self.gone(n - self.dring.shape[0], 0)
        return self.dring.at[s]
    def made(self, b):
        u = len(self.blocks)
        self.blocks.append(b)
        self.born.append(self.n)
        self.send(0, u, 0, self.dring.at[u % self.dring.shape[0], :, self.other], self.cb.at[b], self.partner, self.k)
    def units(self):
        return [(i, u) for i, lag in enumerate(LAGS) for u, t in enumerate(self.born) if t + lag == self.n]
    def before(self):
        for i, u in reversed(self.units()):
            b = self.blocks[u]
            self.arrived(u, (0, 1, 3, 5, 6)[i])
            if i == 0:
                self.mv.start("tc", self.cb.at[b], self.tc)
            elif i == 1:
                self.mv.start("td0", self.dv.at[0, b], self.td.at[0])
                self.mv.start("td1", self.dv.at[1, b], self.td.at[1])
            elif i == 2:
                self.mv.start("te0", self.ev.at[0, b], self.te.at[0])
                self.mv.start("te1", self.ev.at[1, b], self.te.at[1])
            elif i == 3:
                self.mv.start("tf0", self.f1.at[b], self.tf.at[0])
            else:
                self.mv.start("tf1", self.f2.at[b], self.tf.at[1])
    def after(self):
        c, cx, cy, cd, kp, k = self.c, self.cx, self.cy, self.cd, self.kp, self.k
        ns = self.sums.shape[0]
        for i, u in reversed(self.units()):
            b, s = self.blocks[u], self.sums.at[u % ns]
            if i == 0:
                if u >= ns:
                    self.gone(u - ns, 1, 3, 5, 6)
                self.mv.free("tc")
                own = self.dring.at[u % self.dring.shape[0]]
                def one(j):
                    r = rows(j * 96, 96)
                    s[r] = own[r, self.mine] + self.tc[r]
                loop(8, one)
                self.send(1, u, 0, s.at[rows(192 * cd, 96)], self.dv.at[0, b], self.xn, k)
                self.send(1, u, 1, s.at[rows(192 * cd + 96, 96)], self.dv.at[1, b], self.yn, k)
            elif i == 1:
                self.mv.free("td0", "td1")
                r = rows(192 * cy, 96)
                s[r] = s[r] + self.td[0]
                r = rows(192 * cx + 96, 96)
                s[r] = s[r] + self.td[1]
                self.send(3, u, 0, s.at[rows(192 * cx, 192)], self.ev.at[0, b], self.xn, k)
                self.send(3, u, 1, s.at[rows(192 * cy, 192)], self.ev.at[1, b], self.yn, k)
            elif i == 2:
                self.mv.free("te0", "te1")
                def three(j):
                    r, p = rows(192 * c + j * 96, 96), rows(j * 96, 96)
                    s[r] = (s[r].astype(F32) + self.te[0, p].astype(F32) + self.te[1, p].astype(F32)).astype(BF)
                loop(2, three)
                self.send(5, u, 0, s.at[rows(192 * c + 96 * (1 - kp), 96)], self.f1.at[b], self.d, self.peer)
            elif i == 3:
                self.mv.free("tf0")
                r = rows(192 * c + 96 * kp, 96)
                s[r] = s[r] + self.tf[0]
                self.send(6, u, 0, s.at[r], self.f2.at[b], self.d, self.cross)
            else:
                self.mv.free("tf1")
                p = rows(96 * kp, 96)
                self.vv[b, p] = s[rows(192 * c + 96 * kp, 96)] + self.tf[1]
                self.send(7, u, 0, self.vv.at[b, p], self.vv.at[b, p], self.d, self.peer)
        self.n += 1
    def finish(self):
        ns = self.sums.shape[0]
        for u in range(24):
            self.arrived(u, 7)
            self.gone(u, 7)
            if u >= 24 - self.dring.shape[0]:
                self.gone(u, 0)
            if u >= 24 - ns:
                self.gone(u, 1, 3, 5, 6)

def backward_kernel(block_ref, ids_ref, mask_ref, tail_ref, classes_ref, norm_ref, g_ref, head_ref, x0, x1, wall, middles, lns, qkvs, atts, probs_in, hids, slopes,
                    own_ref, tout_ref, mout_ref, cout_ref, cb, dv, ev, f1, f2,
                    g, acc, xs, low, ln, hid, slope, qkv, dqkv, att, probs, ring, dring, sums, tc, td, te, tf, vv,
                    dnorm, tcb, tz, tp, mb, mc, me, mz, kb, sems, red_sems, o_s, o_r,
                    t_s, t_r, tz_s, tz_r, tr_s, tr_r, tg_s, tg_r, m_s, m_r, mr_s, mr_r, mz_s, mz_r, mg_s, mg_r, k_s, k_r, kp_s, kp_r):
    at = place()
    d, k, q, c, cx, cy, cd = at
    barrier(d, k)
    mv = Moves(sems)
    order = []
    for l in reversed(range(LAYERS)):
        for j in range(4):
            order += [12 * l + 8 + j, 12 * l + 4 + j]
        order += [12 * l + 3, 12 * l, 12 * l + 1, 12 * l + 2]
    ws = Weights(mv, wall, ring, order)
    red = Reducer(mv, at, dring, sums, (tc, td, te, tf), vv, (cb, dv, ev, f1, f2), red_sems)
    xn, yn, dn, partner = red.xn, red.yn, cd * 2 + q, red.partner
    mine, other = red.mine, red.other
    started = []
    def go(cp):
        cp.start()
        started.append(cp)
        return cp
    def weight_grad(b, a, cc):
        out = red.slot()
        red.before()
        for n in range(3):
            cs = slice(256 * n, 256 * n + 256)
            out[:, cs] = dot_ta(a[...], cc[:, cs]).astype(BF)
        red.made(b)
        red.after()
    def product(out, a, w, more):
        for n in range(3):
            cs = slice(256 * n, 256 * n + 256)
            v = dot_tb(a[...], w[cs, :])
            out[:, cs] = out[:, cs] + v if more else v
    def chunk(l, j):
        mv.start(("hid", j % 2), hids.at[l, j], hid.at[j % 2])
        mv.start(("slope", j % 2), slopes.at[l, j], slope.at[j % 2])
    gu = dqkv.at[0]
    mv.start("g", g_ref, g)
    chunk(1, 0)
    ws.fill(3)
    for l in reversed(range(LAYERS)):
        base = 12 * l
        mv.start("ln", lns.at[l, 1], ln)
        mv.start("xs", middles.at[l], xs)
        mv.start("att", atts.at[l], att)
        mv.start("probs", probs_in.at[l], probs)
        for j in range(3):
            mv.start(("qkv", j), qkvs.at[l, j], qkv.at[j])
        mv.free("g")
        round_into(low, g)
        mv.free("ln")
        for j in range(4):
            if j < 3:
                chunk(l, j + 1)
            elif l:
                chunk(l - 1, 0)
            mv.free(("hid", j % 2), ("slope", j % 2))
            w = ws.take(base + 8 + j)
            for n in range(3):
                cs = slice(256 * n, 256 * n + 256)
                gu[:, cs] = (dot_tb(low[...], w[cs, :]) * slope[j % 2, :, cs].astype(F32)).astype(BF)
            weight_grad(base + 8 + j, hid.at[j % 2], low)
            product(acc, gu, ws.take(base + 4 + j), j > 0)
            weight_grad(base + 4 + j, ln, gu)
        mv.start("ln", lns.at[l, 0], ln)
        mv.free("xs")
        norm_back(xs, acc, g, g, norm_ref, 4 * l + 2, dnorm)
        mv.start("xs", (x1 if l else x0), xs)
        round_into(low, g)
        mv.free("att")
        weight_grad(base + 3, att, low)
        w = ws.take(base + 3)
        for n in range(3):
            cs = slice(256 * n, 256 * n + 256)
            att[:, cs] = dot_tb(low[...], w[cs, :]).astype(BF)
        mv.free("probs", ("qkv", 0), ("qkv", 1), ("qkv", 2))
        for part in range(2):
            red.before()
            loop(3, lambda i: attend_back(part, i, qkv.at[0], qkv.at[1], qkv.at[2], probs, att, dqkv.at[0], dqkv.at[1], dqkv.at[2]))
            red.after()
        mv.free("ln")
        for j in range(3):
            product(acc, dqkv.at[j], ws.take(base + j), j > 0)
            weight_grad(base + j, ln, dqkv.at[j])
        mv.free("xs")
        norm_back(xs, acc, g, g, norm_ref, 4 * l, dnorm)
    mv.start("acc", head_ref.at[pl.ds(512, 512)], acc.at[pl.ds(0, 512)])
    round_into(low, g)
    for i in range(3):
        row = g[SEQ * i + 256:SEQ * i + 257].astype(BF).astype(F32)
        for t in range(6):
            kb[6 * i + t:6 * i + t + 1] = row[:, 128 * t:128 * t + 128]
    kb[18:24] = classes_ref[0:6]
    cout_ref[k, d] = kb[...]
    kz = [go(remote(kb, cout_ref.at[k, d], k_s.at[i], k_r.at[i], d, (k + i) % 4)) for i in range(1, 4)]
    def position(i):
        r = pl.ds(pl.multiple_of(i * 16, 16), 16)
        xs[r] = g[r] + g[pl.ds(pl.multiple_of(i * 16 + SEQ, 16), 16)] + g[pl.ds(pl.multiple_of(i * 16 + 2 * SEQ, 16), 16)]
    loop(17, position)
    mb[1:257] = xs[0:256]
    mb[0:1] = xs[256:257]
    mb[257:258] = dot(mask_ref[...], low[...])[0:1]
    mb[258:264] = jnp.zeros((6, W), F32)
    mb[264:280] = tail_ref[...]
    mb[265:273] = dnorm[0:8]
    mb[280:288] = jnp.zeros((8, W), F32)
    mcore = go(remote(mb.at[:, other], mc, m_s, m_r, partner, k))
    mv.start("xs", head_ref.at[pl.ds(0, 512)], xs.at[pl.ds(0, 512)])
    red.before()
    red.after()
    mv.free("xs", "acc")
    tcore = []
    for hf in range(2):
        code = lax.broadcasted_iota(jnp.int32, (ROWS, 512), 1) + 512 * hf
        hot = (code == ids_ref[...]).astype(BF)
        part = (xs, acc)[hf]
        buf = dqkv.at[hf]
        for n in range(3):
            cs = slice(256 * n, 256 * n + 256)
            buf[0:512, cs] = (math.sqrt(MODEL_WIDTH) * dot_ta(hot, low[:, cs]) + part[0:512, cs]).astype(BF)
        tcore.append(go(remote(buf.at[pl.ds(0, 512), other], tcb.at[pl.ds(512 * hf, 512)], t_s.at[hf], t_r.at[hf], partner, k)))
    red.before()
    red.after()
    mcore.wait_recv()
    for j in range(4):
        r = pl.ds(j * 72, 72)
        mc[r] = mc[r] + mb[r, mine]
    mr = [go(remote(mc.at[pl.ds(pl.multiple_of(cc * 72, 8), 72)], me.at[j], mr_s.at[j], mr_r.at[j], t, k))
          for j, (cc, t) in enumerate(((cx, xn), (cy, yn), (cd, dn)))]
    for cp in tcore:
        cp.wait_recv()
    for hf in range(2):
        def t_add(i, hf=hf):
            r = rows(i * 64, 64)
            s = rows(512 * hf + i * 64, 64)
            tcb[s] = tcb[s] + dqkv[hf, r, mine]
        loop(8, t_add)
    tzs = [go(remote(tcb.at[rows(((k + i) % 4) * 256, 256)], tz.at[i - 1], tz_s.at[i], tz_r.at[i], d, (k + i) % 4)) for i in range(1, 4)]
    red.before()
    red.after()
    for cp in kz:
        cp.wait_recv()
    kps = [go(remote(cout_ref.at[:, d], cout_ref.at[:, d], kp_s.at[i], kp_r.at[i], (d + i) % 8, k)) for i in range(1, 8)]
    for cp in mr:
        cp.wait_recv()
    mz[k] = mc[pl.ds(pl.multiple_of(c * 72, 8), 72)] + me[0] + me[1] + me[2]
    mzs = [go(remote(mz.at[k], mz.at[k], mz_s.at[i], mz_r.at[i], d, (k + i) % 4)) for i in range(1, 4)]
    while red.n <= red.born[-1] + LAGS[-1]:
        red.before()
        red.after()
    for cp in mzs:
        cp.wait_recv()
    r = pl.ds(pl.multiple_of(c * 72, 8), 72)
    mout_ref[r, mine] = (mz[0] + mz[1]) + (mz[2] + mz[3])
    reg = mout_ref.at[r, mine]
    mgs = [go(remote(reg, reg, mg_s.at[j], mg_r.at[j], t, k)) for j, t in enumerate((xn, yn, dn))]
    for cp in tzs:
        cp.wait_recv()
    def t_sum(i):
        r = rows(i * 64, 64)
        s = rows(256 * k + i * 64, 64)
        tcb[s] = (tcb[s].astype(F32) + tz[0, r].astype(F32) + tz[1, r].astype(F32) + tz[2, r].astype(F32)).astype(BF)
    loop(4, t_sum)
    trs = [go(remote(tcb.at[rows(256 * k + 64 * cc, 64)], tp.at[j], tr_s.at[j], tr_r.at[j], t, k))
           for j, (cc, t) in enumerate(((cx, xn), (cy, yn), (cd, dn)))]
    red.finish()
    outs = []
    for i in (4, 5, 6, 7, 2, 3, 1, 0):
        o = (d + i) % 8
        s = i // 2
        cols = slice(HALF * (i % 2), HALF * (i % 2) + HALF)
        for j in range(4):
            ring[s, 192 * j:192 * j + 192, cols] = vv[block_ref[o * 4 + j]]
        for j in range(4):
            src = ring.at[s, pl.ds(192 * j, 192), cols]
            dst = own_ref.at[j, rows(192 * c, 192), mine]
            if i:
                outs.append(go(remote(src, dst, o_s.at[i, j], o_r.at[i, j], o, k)))
            else:
                mv.start(("own", j), src, dst)
    for cp in trs:
        cp.wait_recv()
    tout_ref[rows(64 * c, 64), mine] = (tcb[rows(256 * k + 64 * c, 64)].astype(F32) + tp[0].astype(F32) + tp[1].astype(F32) + tp[2].astype(F32))
    reg = tout_ref.at[rows(64 * c, 64), mine]
    tgs = [go(remote(reg, reg, tg_s.at[j], tg_r.at[j], t, k)) for j, t in enumerate((xn, yn, dn))]
    for cp in mgs + tgs:
        cp.wait_recv()
    reg = tout_ref.at[:, mine]
    last = [go(remote(reg, reg, tg_s.at[3], tg_r.at[3], partner, k))]
    reg = mout_ref.at[:, mine]
    last.append(go(remote(reg, reg, mg_s.at[3], mg_r.at[3], partner, k)))
    for cp in kps + outs + last:
        cp.wait_recv()
    for cp in started:
        cp.wait_send()
    mv.free()

def backward(block_of, ids, mask_row, tail, class_ids, norms, g, head, x0, x1, wall, middles, lns, qkvs, atts, probs, hids, slopes):
    S = jax.ShapeDtypeStruct
    V = pltpu.VMEM
    D = pltpu.SemaphoreType.DMA
    any_ = pl.BlockSpec(memory_space=pl.ANY)
    vm = pl.BlockSpec(memory_space=pltpu.VMEM)
    f32, bf = V((ROWS, W), F32), V((ROWS, W), BF)
    out = pl.pallas_call(
        backward_kernel,
        out_shape=(S((4, W, W), BF), S((256, W), F32), S((288, W), F32), S((4, 8, 24, 128), F32), S((24, W, HALF), BF),
                   S((2, 24, 96, HALF), BF), S((2, 24, 192, HALF), BF), S((24, 96, HALF), BF), S((24, 96, HALF), BF)),
        in_specs=[pl.BlockSpec(memory_space=pltpu.SMEM)] + [vm] * 5 + [any_] * 12, out_specs=(any_, vm, vm, vm) + (any_,) * 5,
        scratch_shapes=[f32, f32, f32, bf, bf, V((2, ROWS, W), BF), V((2, ROWS, W), BF), V((3, ROWS, W), BF), V((3, ROWS, W), BF), bf,
                        V((3, 8, SEQ, SEQ), BF), V((4, W, W), BF), V((4, W, W), BF), V((10, W, HALF), BF),
                        V((W, HALF), BF), V((2, 96, HALF), BF), V((2, 192, HALF), BF), V((2, 96, HALF), BF), V((24, 192, HALF), BF),
                        V((16, W), F32), V((1024, HALF), BF), V((3, 256, HALF), BF), V((3, 64, HALF), BF),
                        V((288, W), F32), V((288, HALF), F32), V((3, 72, HALF), F32), V((4, 72, HALF), F32), V((24, 128), F32),
                        D((48,)), D((2, 192)), D((8, 4)), D((8, 4)),
                        D((2,)), D((2,)), D((4,)), D((4,)), D((3,)), D((3,)), D((4,)), D((4,)), D, D, D((3,)), D((3,)), D((4,)), D((4,)), D((4,)), D((4,)),
                        D((4,)), D((4,)), D((8,)), D((8,))],
        compiler_params=pltpu.CompilerParams(collective_id=1, has_side_effects=True, vmem_limit_bytes=62 * 2**20),
        cost_estimate=pl.CostEstimate(flops=24 * 4 * ROWS * W * W, bytes_accessed=150 * 10**6, transcendentals=10**7),
        name="layers_back",
    )(block_of, ids, mask_row, tail, class_ids, norms, g, head, x0, x1, wall, middles, lns, qkvs, atts, probs, hids, slopes)
    return out[:4]


def norm_rows(inputs, norm_gain, norm_shift):
    row_mean = jnp.mean(inputs, -1, keepdims=True)
    centred = inputs - row_mean
    spread = jnp.mean(centred * centred, -1, keepdims=True)
    return centred * lax.rsqrt(spread + NORM_EPS) * norm_gain + norm_shift


def exact_gelu(inputs):
    return jax.nn.gelu(inputs, approximate=False)


def split_heads(inputs, images):
    return inputs.reshape(images, -1, HEADS, HEAD_DIM)


def attention_scores(queries, key_heads):
    return jnp.einsum(
        "bqhd,bkhd->bhqk", queries, key_heads, preferred_element_type=jnp.float32
    ) * HEAD_DIM ** (-0.5)


def adam_update(weight, moment_one, moment_two, gradient, step_rate, step_float):
    moment_one = BETA_ONE * moment_one + (1.0 - BETA_ONE) * gradient
    moment_two = BETA_TWO * moment_two + (1.0 - BETA_TWO) * gradient * gradient
    fix_one = 1.0 - BETA_ONE**step_float
    fix_two = 1.0 - BETA_TWO**step_float
    weight = weight - step_rate * (
        moment_one / fix_one / (jnp.sqrt(moment_two / fix_two) + ADAM_EPS) + DECAY * weight
    )
    return (weight, moment_one, moment_two)


def layer_forward(stream, layer_weights, norm_gains, images):
    pieces = FF // MODEL_WIDTH
    row_count = stream.shape[0]
    attn_in = norm_rows(stream, norm_gains[0], norm_gains[1]).astype(jnp.bfloat16)
    triple = jnp.einsum(
        "td,jde->jte", attn_in, layer_weights[0:3], preferred_element_type=jnp.float32
    ).astype(jnp.bfloat16)
    scores = attention_scores(split_heads(triple[0], images), split_heads(triple[1], images))
    row_top = jnp.max(scores, -1, keepdims=True)
    expo = jnp.exp(scores - row_top)
    row_total = jnp.sum(expo, -1, keepdims=True)
    probs_low = (expo / row_total).astype(jnp.bfloat16)
    log_total = row_top + jnp.log(row_total)
    attended = (
        jnp.einsum(
            "bhqk,bkhd->bqhd",
            probs_low,
            split_heads(triple[2], images),
            preferred_element_type=jnp.float32,
        )
        .reshape(row_count, MODEL_WIDTH)
        .astype(jnp.bfloat16)
    )
    middle = stream + jnp.dot(attended, layer_weights[3], preferred_element_type=jnp.float32)
    mlp_in = norm_rows(middle, norm_gains[2], norm_gains[3]).astype(jnp.bfloat16)
    up_proj = jnp.einsum(
        "td,jde->tje", mlp_in, layer_weights[4 : 4 + pieces], preferred_element_type=jnp.float32
    ).reshape(row_count, FF)
    hidden = exact_gelu(up_proj).astype(jnp.bfloat16)
    down_out = jnp.einsum(
        "tjd,jde->te",
        hidden.reshape(row_count, pieces, MODEL_WIDTH),
        layer_weights[4 + pieces : 4 + 2 * pieces],
        preferred_element_type=jnp.float32,
    )
    return (
        middle + down_out,
        (stream, attn_in, triple, log_total, attended, middle, mlp_in, up_proj, hidden),
    )


def layer_backward(grad_out, layer_weights, norm_gains, saved_values, images):
    stream, attn_in, triple, log_total, attended, middle, mlp_in, up_proj, hidden = saved_values
    pieces = FF // MODEL_WIDTH
    row_count = stream.shape[0]
    branch = grad_out.astype(jnp.bfloat16)
    grad_hidden = jnp.einsum(
        "te,jde->tjd",
        branch,
        layer_weights[4 + pieces : 4 + 2 * pieces],
        preferred_element_type=jnp.float32,
    ).reshape(row_count, FF)
    grad_down = jnp.einsum(
        "tjd,te->jde",
        hidden.reshape(row_count, pieces, MODEL_WIDTH),
        branch,
        preferred_element_type=jnp.float32,
    )
    grad_upper = (
        jax.vjp(exact_gelu, up_proj)[1](grad_hidden)[0]
        .astype(jnp.bfloat16)
        .reshape(row_count, pieces, MODEL_WIDTH)
    )
    grad_up = jnp.einsum("td,tje->jde", mlp_in, grad_upper, preferred_element_type=jnp.float32)
    grad_mlp_in = jnp.einsum(
        "tje,jde->td", grad_upper, layer_weights[4 : 4 + pieces], preferred_element_type=jnp.float32
    )
    grad_mid_norm, grad_gain_two, grad_shift_two = jax.vjp(
        norm_rows, middle, norm_gains[2], norm_gains[3]
    )[1](grad_mlp_in)
    grad_middle = grad_out + grad_mid_norm
    branch = grad_middle.astype(jnp.bfloat16)
    grad_out_proj = jnp.einsum("td,te->de", attended, branch, preferred_element_type=jnp.float32)
    grad_attended = split_heads(
        jnp.einsum(
            "te,de->td", branch, layer_weights[3], preferred_element_type=jnp.float32
        ).astype(jnp.bfloat16),
        images,
    )
    queries = split_heads(triple[0], images)
    key_heads = split_heads(triple[1], images)
    value_heads = split_heads(triple[2], images)
    attn_probs = jnp.exp(attention_scores(queries, key_heads) - log_total)
    grad_probs = jnp.einsum(
        "bqhd,bkhd->bhqk", grad_attended, value_heads, preferred_element_type=jnp.float32
    )
    grad_scores = (
        attn_probs * (grad_probs - jnp.sum(attn_probs * grad_probs, -1, keepdims=True))
    ).astype(jnp.bfloat16)
    score_scale = HEAD_DIM ** (-0.5)
    grad_query = (
        jnp.einsum("bhqk,bkhd->bqhd", grad_scores, key_heads, preferred_element_type=jnp.float32)
        * score_scale
    )
    grad_keys = (
        jnp.einsum("bhqk,bqhd->bkhd", grad_scores, queries, preferred_element_type=jnp.float32)
        * score_scale
    )
    grad_values = jnp.einsum(
        "bhqk,bqhd->bkhd",
        attn_probs.astype(jnp.bfloat16),
        grad_attended,
        preferred_element_type=jnp.float32,
    )
    grad_triple = (
        jnp.stack([grad_query, grad_keys, grad_values])
        .reshape(3, row_count, MODEL_WIDTH)
        .astype(jnp.bfloat16)
    )
    grad_qkv = jnp.einsum("td,jte->jde", attn_in, grad_triple, preferred_element_type=jnp.float32)
    grad_attn_in = jnp.einsum(
        "jte,jde->td", grad_triple, layer_weights[0:3], preferred_element_type=jnp.float32
    )
    grad_in_norm, grad_gain_one, grad_shift_one = jax.vjp(
        norm_rows, stream, norm_gains[0], norm_gains[1]
    )[1](grad_attn_in)
    gradients = jnp.concatenate([grad_qkv, grad_out_proj[None], grad_up, grad_down], axis=0)
    norm_grads = jnp.stack([grad_gain_one, grad_shift_one, grad_gain_two, grad_shift_two])
    return (grad_middle + grad_in_norm, gradients, norm_grads)


def pick(blocks, order):
    return jnp.stack(
        [lax.dynamic_index_in_dim(blocks, order[i], 0, keepdims=False) for i in range(order.shape[0])]
    )


def on_device(
    code_ids,
    masked,
    labels,
    dropped,
    owners,
    step_count,
    master_block_weight,
    matrix_first_moment,
    matrix_second_moment,
    embed_weight,
    embed_first,
    embed_second,
    extra_weight,
    extra_first,
    extra_second,
    norm_weight,
    norm_first,
    norm_second,
    bias_weight,
    bias_first,
    bias_second,
):
    images = code_ids.shape[0]
    seq_len = IMAGE_TOKENS + 1
    slot_count = master_block_weight.shape[0]
    block_count = owners.shape[0]
    per_layer = BLOCKS // LAYERS
    block_index = jnp.arange(block_count)
    same_owner = (owners[None, :] == owners[:, None]) & (
        block_index[None, :] < block_index[:, None]
    )
    owner_rank = jnp.sum(same_owner.astype(jnp.int32), axis=1)
    slot_of = owners * slot_count + owner_rank
    slot_index = jnp.arange(slot_count * lax.axis_size("dp"))
    slot_match = slot_of[None, :] == slot_index[:, None]
    filled = jnp.any(slot_match, axis=1)
    block_of = jnp.sum(jnp.where(slot_match, block_index[None, :], 0), axis=1)
    mask_float = masked.astype(jnp.float32)
    count = jnp.broadcast_to(jnp.sum(mask_float), (8, 128))
    classes = jnp.where(dropped == 1, CLASSES, labels)
    own_rows = images * IMAGE_TOKENS
    room = ((0, 0), (0, SEQ - IMAGE_TOKENS))
    kept_ids = jnp.pad(jnp.where(masked == 1, -1, code_ids), room, constant_values=-1).reshape(ROWS, 1)
    mask_padded = jnp.pad(mask_float, room)
    positions = jnp.concatenate(
        [
            extra_weight[1:seq_len],
            extra_weight[:1],
            jnp.zeros((SEQ - REAL, MODEL_WIDTH), jnp.float32),
        ]
    )
    few = jnp.concatenate(
        [
            lax.dynamic_index_in_dim(extra_weight, IMAGE_TOKENS + 2 + classes[i], 0, keepdims=True)
            for i in range(3)
        ]
        + [extra_weight[IMAGE_TOKENS + 1][None], jnp.zeros((4, MODEL_WIDTH), jnp.float32)]
    )
    norms = jnp.pad(norm_weight, ((0, 6), (0, 0)))
    all_weights, code_table, masked_total, first, stream1, stream2, *saved = forward(
        slot_of, chunks_to_send(master_block_weight), embed_weight.astype(BF), count,
        kept_ids, mask_padded.reshape(ROWS, 1), positions, few, norms,
    )
    inverse = 1.0 / masked_total[0, 0]
    flat_codes = code_ids.reshape(own_rows)
    code_hot = (flat_codes[:, None] == jnp.arange(CODES)[None, :]).astype(BF)
    target_rows = jnp.dot(code_hot, code_table, preferred_element_type=jnp.float32)
    stream = stream2.reshape(images, SEQ, MODEL_WIDTH)[:, :IMAGE_TOKENS].reshape(own_rows, MODEL_WIDTH)
    final_gain = norm_weight[4 * LAYERS]
    final_shift = norm_weight[4 * LAYERS + 1]
    code_final = norm_rows(stream, final_gain, final_shift).astype(BF)
    flat_mask = mask_float.reshape(own_rows)
    logits = (
        jnp.einsum("td,cd->tc", code_final, code_table, preferred_element_type=jnp.float32)
        + bias_weight
    )
    row_top = jnp.max(logits, axis=1)
    log_total = row_top + jnp.log(jnp.sum(jnp.exp(logits - row_top[:, None]), axis=1))
    weighted = jnp.exp(logits - log_total[:, None]) * (flat_mask * inverse)[:, None]
    grad_logits = weighted.astype(jnp.bfloat16)
    own_weight = flat_mask * inverse
    target_logit = (
        jnp.sum(code_final.astype(jnp.float32) * target_rows, axis=1)
        + jnp.sum(jnp.where(flat_codes[:, None] == jnp.arange(CODES)[None, :], bias_weight, 0.0), axis=1)
    )
    loss_part = jnp.sum(own_weight * (log_total - target_logit))
    grad_code = jnp.dot(grad_logits, code_table, preferred_element_type=jnp.float32)
    grad_code = grad_code - own_weight[:, None] * target_rows
    head_table = jnp.einsum(
        "tc,td->cd", grad_logits, code_final, preferred_element_type=jnp.float32
    )
    head_bias = jnp.sum(weighted, axis=0)
    grad_stream, grad_gain, grad_shift = jax.vjp(norm_rows, stream, final_gain, final_shift)[1](
        grad_code
    )
    grad_stream = jnp.pad(
        grad_stream.reshape(images, IMAGE_TOKENS, MODEL_WIDTH), ((0, 0), (0, SEQ - IMAGE_TOKENS), (0, 0))
    ).reshape(ROWS, MODEL_WIDTH)
    masked_hot = code_hot * flat_mask[:, None].astype(jnp.bfloat16)
    target_term = jnp.dot(masked_hot.T, code_final, preferred_element_type=jnp.float32)
    head_term = head_table - inverse * target_term
    bias_grad = head_bias - inverse * jnp.sum(masked_hot.astype(jnp.float32), axis=0)
    tail = jnp.concatenate(
        [
            jnp.zeros((9, MODEL_WIDTH), jnp.float32),
            grad_gain[None],
            grad_shift[None],
            jnp.pad(bias_grad, (0, 2 * MODEL_WIDTH - CODES)).reshape(2, MODEL_WIDTH),
            jnp.full((1, MODEL_WIDTH), loss_part),
            jnp.zeros((2, MODEL_WIDTH), jnp.float32),
        ]
    )
    mask_row = jnp.pad(mask_padded.reshape(1, ROWS), ((0, 15), (0, 0))).astype(BF)
    class_pack = jnp.pad(classes.astype(jnp.float32)[None], ((0, 7), (0, 125)))
    owned, table_grad, misc, class_all = backward(
        block_of, kept_ids, mask_row, tail, class_pack, norms, grad_stream, head_term,
        first, stream1, all_weights.reshape(BLOCKS, MODEL_WIDTH, MODEL_WIDTH), *saved
    )
    owned = owned.astype(jnp.float32)
    class_rows = class_all[:, :, :18].reshape(-1, MODEL_WIDTH).astype(BF)
    class_ids = class_all[:, :, 18, :3].reshape(-1) + (seq_len + 1.0)
    class_hot = (class_ids[:, None] == jnp.arange(extra_weight.shape[0]).astype(jnp.float32)).astype(BF)
    class_grad = jnp.dot(class_hot.T, class_rows, preferred_element_type=jnp.float32)
    extra_grad = class_grad + jnp.pad(
        misc[: seq_len + 1], ((0, extra_weight.shape[0] - seq_len - 1), (0, 0))
    )
    norm_grad = misc[265:275]
    bias_grad = misc[275:277].reshape(-1)[:CODES]
    step_loss = misc[277, 0]
    own_filled = lax.dynamic_slice_in_dim(filled, lax.axis_index("dp") * slot_count, slot_count)[
        :, None, None
    ]
    step_float = step_count[0].astype(jnp.float32)
    block_new = adam_update(
        master_block_weight, matrix_first_moment, matrix_second_moment, owned, 0.03, step_float
    )
    table_new = adam_update(embed_weight, embed_first, embed_second, table_grad, 0.05, step_float)
    extra_new = adam_update(extra_weight, extra_first, extra_second, extra_grad, 0.5, step_float)
    norm_new = adam_update(norm_weight, norm_first, norm_second, norm_grad, 0.5, step_float)
    bias_new = adam_update(bias_weight, bias_first, bias_second, bias_grad, 0.3, step_float)
    return (
        step_loss,
        jnp.where(own_filled, block_new[0], 0.0),
        jnp.where(own_filled, block_new[1], 0.0),
        jnp.where(own_filled, block_new[2], 0.0),
        table_new[0],
        table_new[1],
        table_new[2],
        extra_new[0],
        extra_new[1],
        extra_new[2],
        norm_new[0],
        norm_new[1],
        norm_new[2],
        bias_new[0],
        bias_new[1],
        bias_new[2],
    )


def any_mesh(
    code_ids,
    masked,
    labels,
    dropped,
    owners,
    step_count,
    master_block_weight,
    matrix_first_moment,
    matrix_second_moment,
    embed_weight,
    embed_first,
    embed_second,
    extra_weight,
    extra_first,
    extra_second,
    norm_weight,
    norm_first,
    norm_second,
    bias_weight,
    bias_first,
    bias_second,
):
    images = code_ids.shape[0]
    seq_len = IMAGE_TOKENS + 1
    slot_count = master_block_weight.shape[0]
    block_count = owners.shape[0]
    per_layer = BLOCKS // LAYERS
    block_index = jnp.arange(block_count)
    same_owner = (owners[None, :] == owners[:, None]) & (
        block_index[None, :] < block_index[:, None]
    )
    owner_rank = jnp.sum(same_owner.astype(jnp.int32), axis=1)
    slot_of = owners * slot_count + owner_rank
    slot_index = jnp.arange(slot_count * lax.axis_size("dp"))
    slot_match = slot_of[None, :] == slot_index[:, None]
    filled = jnp.any(slot_match, axis=1)
    block_of = jnp.sum(jnp.where(slot_match, block_index[None, :], 0), axis=1)
    gathered = lax.all_gather(master_block_weight.astype(jnp.bfloat16), "dp", axis=0, tiled=True)
    all_weights = pick(gathered, slot_of)
    local_table = embed_weight.astype(jnp.bfloat16)
    code_table = lax.all_gather(local_table, "vocab", axis=0, tiled=True)
    mask_float = masked.astype(jnp.float32)
    masked_total = lax.psum(jnp.sum(mask_float), ("dp", "vocab"))
    inverse = 1.0 / masked_total
    classes = jnp.where(dropped == 1, CLASSES, labels)
    code_rows = jnp.where(
        mask_float[..., None] > 0,
        extra_weight[IMAGE_TOKENS + 1],
        math.sqrt(MODEL_WIDTH) * jnp.take(code_table, code_ids, axis=0).astype(jnp.float32),
    )
    class_rows = jnp.take(extra_weight, IMAGE_TOKENS + 2 + classes, axis=0)
    stream = (
        jnp.concatenate([class_rows[:, None], code_rows], axis=1) + extra_weight[:seq_len]
    ).reshape(images * seq_len, MODEL_WIDTH)
    saved_layers = []
    for layer_index in range(LAYERS):
        stream, saved_values = layer_forward(
            stream,
            all_weights[per_layer * layer_index : per_layer * (layer_index + 1)],
            norm_weight[4 * layer_index : 4 * layer_index + 4],
            images,
        )
        saved_layers.append(saved_values)
    final_gain = norm_weight[4 * LAYERS]
    final_shift = norm_weight[4 * LAYERS + 1]
    final_rows = norm_rows(stream, final_gain, final_shift)
    own_rows = images * IMAGE_TOKENS
    code_final = (
        final_rows.reshape(images, seq_len, MODEL_WIDTH)[:, 1:]
        .reshape(own_rows, MODEL_WIDTH)
        .astype(jnp.bfloat16)
    )
    flat_mask = mask_float.reshape(own_rows)
    group_rows, group_mask = (
        lax.all_gather(code_final, "vocab", axis=0, tiled=True),
        lax.all_gather(flat_mask.astype(jnp.bfloat16), "vocab", axis=0, tiled=True),
    )
    shard_codes = local_table.shape[0]
    vocab_index = lax.axis_index("vocab")
    local_bias = lax.dynamic_slice_in_dim(bias_weight, vocab_index * shard_codes, shard_codes)
    logits = (
        jnp.einsum("td,cd->tc", group_rows, local_table, preferred_element_type=jnp.float32)
        + local_bias
    )
    row_top = jnp.max(logits, axis=1)
    row_total = jnp.sum(jnp.exp(logits - row_top[:, None]), axis=1)
    group_top = lax.pmax(row_top, "vocab")
    group_total = lax.psum(row_total * jnp.exp(row_top - group_top), "vocab")
    log_total = group_top + jnp.log(group_total)
    row_weight = group_mask.astype(jnp.float32) * inverse
    weighted = jnp.exp(logits - log_total[:, None]) * row_weight[:, None]
    grad_logits = weighted.astype(jnp.bfloat16)
    flat_codes = code_ids.reshape(own_rows)
    target_rows = jnp.take(code_table, flat_codes, axis=0)
    own_weight = flat_mask * inverse
    target_logit = (
        jnp.sum(code_final.astype(jnp.float32) * target_rows.astype(jnp.float32), axis=1)
        + bias_weight[flat_codes]
    )
    own_log_total = lax.dynamic_slice_in_dim(log_total, vocab_index * own_rows, own_rows)
    loss_part = jnp.sum(own_weight * (own_log_total - target_logit))
    grad_code = lax.psum_scatter(
        jnp.dot(grad_logits, local_table, preferred_element_type=jnp.float32).astype(jnp.bfloat16),
        "vocab",
        scatter_dimension=0,
        tiled=True,
    ).astype(jnp.float32)
    grad_code = grad_code - own_weight[:, None] * target_rows.astype(jnp.float32)
    head_table = jnp.einsum(
        "tc,td->cd", grad_logits, group_rows, preferred_element_type=jnp.float32
    )
    head_bias = jnp.sum(weighted, axis=0)
    grad_final = jnp.concatenate(
        [
            jnp.zeros((images, 1, MODEL_WIDTH), jnp.float32),
            grad_code.reshape(images, IMAGE_TOKENS, MODEL_WIDTH),
        ],
        axis=1,
    ).reshape(images * seq_len, MODEL_WIDTH)
    grad_stream, grad_gain, grad_shift = jax.vjp(norm_rows, stream, final_gain, final_shift)[1](
        grad_final
    )
    layer_grads = []
    gain_grads = []
    for layer_index in reversed(range(LAYERS)):
        grad_stream, block_grads, norm_grads = layer_backward(
            grad_stream,
            all_weights[per_layer * layer_index : per_layer * (layer_index + 1)],
            norm_weight[4 * layer_index : 4 * layer_index + 4],
            saved_layers[layer_index],
            images,
        )
        layer_grads.insert(0, block_grads)
        gain_grads.insert(0, norm_grads)
    all_grads = jnp.concatenate(layer_grads, axis=0)
    norm_grad = jnp.concatenate(gain_grads + [jnp.stack([grad_gain, grad_shift])], axis=0)
    token_low = lax.optimization_barrier(grad_stream.astype(jnp.bfloat16)).reshape(
        images, seq_len, MODEL_WIDTH
    )
    token_grad = token_low.astype(jnp.float32)
    position_grad = jnp.sum(grad_stream.reshape(images, seq_len, MODEL_WIDTH), axis=0)
    mask_grad = jnp.sum(mask_float[..., None] * token_grad[:, 1:], axis=(0, 1))
    class_hot = (classes[:, None] == jnp.arange(CLASSES + 1)[None, :]).astype(jnp.bfloat16)
    class_grad = jnp.dot(class_hot.T, token_low[:, 0], preferred_element_type=jnp.float32)
    extra_grad = jnp.concatenate([position_grad, mask_grad[None], class_grad], axis=0)
    code_hot = (flat_codes[:, None] == jnp.arange(CODES)[None, :]).astype(jnp.bfloat16)
    kept_hot = code_hot * (1.0 - flat_mask)[:, None].astype(jnp.bfloat16)
    masked_hot = code_hot * flat_mask[:, None].astype(jnp.bfloat16)
    input_term = jnp.dot(
        kept_hot.T,
        token_low[:, 1:].reshape(own_rows, MODEL_WIDTH),
        preferred_element_type=jnp.float32,
    )
    target_term = jnp.dot(masked_hot.T, code_final, preferred_element_type=jnp.float32)
    table_term = math.sqrt(MODEL_WIDTH) * input_term - inverse * target_term
    table_piece = (
        lax.psum_scatter(
            table_term.astype(jnp.bfloat16), "vocab", scatter_dimension=0, tiled=True
        ).astype(jnp.float32)
        + head_table
    )
    table_grad = lax.psum(table_piece, "dp")
    placed_bias = lax.dynamic_update_slice_in_dim(
        jnp.zeros((CODES,), jnp.float32), head_bias, vocab_index * shard_codes, 0
    )
    bias_grad = placed_bias - inverse * jnp.sum(masked_hot.astype(jnp.float32), axis=0)
    step_loss, extra_grad, norm_grad, bias_grad = lax.psum(
        (loss_part, extra_grad, norm_grad, bias_grad), ("dp", "vocab")
    )
    owned = lax.psum_scatter(
        jnp.where(filled[:, None, None], pick(all_grads, block_of), 0.0).astype(
            jnp.bfloat16
        ),
        "dp",
        scatter_dimension=0,
        tiled=True,
    ).astype(jnp.float32)
    owned = lax.psum(owned, "vocab")
    own_filled = lax.dynamic_slice_in_dim(filled, lax.axis_index("dp") * slot_count, slot_count)[
        :, None, None
    ]
    step_float = step_count[0].astype(jnp.float32)
    block_new = adam_update(
        master_block_weight, matrix_first_moment, matrix_second_moment, owned, 0.03, step_float
    )
    table_new = adam_update(embed_weight, embed_first, embed_second, table_grad, 0.05, step_float)
    extra_new = adam_update(extra_weight, extra_first, extra_second, extra_grad, 0.5, step_float)
    norm_new = adam_update(norm_weight, norm_first, norm_second, norm_grad, 0.5, step_float)
    bias_new = adam_update(bias_weight, bias_first, bias_second, bias_grad, 0.3, step_float)
    return (
        step_loss,
        jnp.where(own_filled, block_new[0], 0.0),
        jnp.where(own_filled, block_new[1], 0.0),
        jnp.where(own_filled, block_new[2], 0.0),
        table_new[0],
        table_new[1],
        table_new[2],
        extra_new[0],
        extra_new[1],
        extra_new[2],
        norm_new[0],
        norm_new[1],
        norm_new[2],
        bias_new[0],
        bias_new[1],
        bias_new[2],
    )


def solution(mesh):
    placed = (
        P(("dp", "vocab"), None),
        P(("dp", "vocab"), None),
        P(("dp", "vocab")),
        P(("dp", "vocab")),
        P(),
        P(),
        P("dp", None, None),
        P("dp", None, None),
        P("dp", None, None),
        P("vocab", None),
        P("vocab", None),
        P("vocab", None),
        P(),
        P(),
        P(),
        P(),
        P(),
        P(),
        P(),
        P(),
        P(),
    )
    fast = mesh.shape["dp"] == 8 and mesh.shape["vocab"] == 4
    return jax.shard_map(
        on_device if fast else any_mesh,
        mesh=mesh,
        in_specs=placed,
        out_specs=(
            P(),
            P("dp", None, None),
            P("dp", None, None),
            P("dp", None, None),
            P("vocab", None),
            P("vocab", None),
            P("vocab", None),
            P(),
            P(),
            P(),
            P(),
            P(),
            P(),
            P(),
            P(),
            P(),
        ),
        check_vma=False,
    )
```
